256 devices in a mesh: orb: 64 (over x, z, core), aux: 4 (over y).
Axes of the slice: x: 4, y: 4, z: 8, core: 2. Of those that a mesh axis runs over, the one named last changes fastest.
Arguments:
- tensor: bfloat16 [30720, 2, 64, 256], P('aux', None, 'orb'), may hold values from -6 to 6
- density: bfloat16 [64, 512, 512], P('orb'), may hold values from -0.375 to 0.375
- block_ids: int32 [2, 64, 4], P(None, 'orb'), may hold values from 0 to 7
- counts: int32 [2, 64], P(None, 'orb'), may hold values from 1 to 4
Outputs:
- panel: float32 [64, 30720], P(None, ('aux', 'orb'))
The draws below stay inside these ranges and needn't reach their ends.
All inputs are finite; a program needn't handle non-finite values.
Results may differ from the reference program's by a relative error of at most 0.0029.
Values may be sent and summed in bfloat16 or wider, within the bound.
A program may use at most 128 MiB of HBM per device.

```python
import math
import jax
import jax.numpy as jnp
from jax import lax

NAUX = 30720
BLK = 64
SLOTS = 4
WIN = 8
SLABS = 2
PANEL = 64
NORB = 64


def place_ends(result, rng, smallest, largest):
    extent = result.shape
    place = [jax.random.randint(jax.random.fold_in(rng, axis), (), 0, extent[axis]) for axis in range(len(extent))]
    result = result.at[tuple(place)].set(smallest)
    longest = extent.index(max(extent))
    place[longest] = (place[longest] + 1) % extent[longest]
    return result.at[tuple(place)].set(largest)


def levels(rng, dims, split, smallest, top_value):
    gain, own = 1.0, jax.random.fold_in(rng, 6)
    for position, shards_of in split:
        draws = jnp.exp(jax.random.uniform(jax.random.fold_in(own, position), (shards_of,), jnp.float32, smallest / len(split), top_value / len(split)))
        gain = gain * jnp.repeat(draws, dims[position] // shards_of).reshape([-1 if axis == position else 1 for axis in range(len(dims))])
    return gain


def centred(stream_key, extent, spread, bound, cuts=(), kind=jnp.bfloat16):
    array = spread * jax.random.normal(stream_key, extent, jnp.float32)
    if cuts:
        array = array * levels(stream_key, extent, cuts, -0.22, 0.18)
    return jnp.clip(array, -bound, bound).astype(kind)


def setup_inputs(seed: int = 0) -> dict:
    splits = jax.random.split(jax.random.key(seed), 5)
    return {
        "tensor": centred(splits[0], (NAUX, SLABS, NORB, SLOTS * BLK), 1.0, 6.0, ((0, 4), (2, 64))),
        "density": centred(splits[1], (NORB, WIN * BLK, WIN * BLK), (SLOTS * BLK) ** -0.5, 0.375, ((0, 64),)),
        "block_ids": place_ends(jax.random.randint(splits[2], (SLABS, NORB, SLOTS), 0, WIN), jax.random.fold_in(splits[2], 1), 0, WIN - 1).astype(jnp.int32),
        "counts": place_ends(jax.random.randint(splits[3], (SLABS, NORB), 1, SLOTS + 1), jax.random.fold_in(splits[3], 1), 1, SLOTS).astype(jnp.int32),
    }


def reference(tensor, density, block_ids, counts):
    slot_range = jnp.arange(SLOTS, dtype=jnp.int32)
    window_range = jnp.arange(WIN, dtype=jnp.int32)
    factor = 1.0 / math.sqrt(SLABS * NORB * SLOTS * BLK)

    def orbital_term(carry, orbital):
        chosen = lax.dynamic_index_in_dim(tensor, orbital, 2, keepdims=False)
        slot_count = lax.dynamic_index_in_dim(counts, orbital, 1, keepdims=False)
        live_slots = slot_range[None, :] < slot_count[:, None]
        column_live = jnp.repeat(live_slots, BLK, axis=1)
        masked = jnp.where(column_live[None], chosen, jnp.zeros((), jnp.bfloat16))
        tile_grid = lax.dynamic_index_in_dim(density, orbital, 0, keepdims=False).astype(jnp.float32)
        tile_grid = tile_grid.reshape(WIN, BLK, WIN, BLK)
        chosen_ids = lax.dynamic_index_in_dim(block_ids, orbital, 1, keepdims=False)
        selector = (chosen_ids[:, :, None] == window_range[None, None, :]).astype(jnp.float32)
        local_density = jnp.einsum('ksw,wixj,ktx->ksitj', selector, tile_grid, selector, precision=lax.Precision.HIGHEST).reshape(SLABS, SLOTS * BLK, SLOTS * BLK)
        mixed_rows = jnp.einsum('rkc,kcd->rkd', masked.astype(jnp.float32), local_density, precision=lax.Precision.HIGHEST).astype(jnp.bfloat16)
        mixed_rows = lax.optimization_barrier(mixed_rows)
        panel_term = jnp.einsum('pkc,rkc->pr', masked[:PANEL].astype(jnp.float32), mixed_rows.astype(jnp.float32), precision=lax.Precision.HIGHEST)
        return (carry + panel_term * factor, None)
    start = jnp.zeros((PANEL, NAUX), jnp.float32)
    total, _ = lax.scan(orbital_term, start, jnp.arange(NORB, dtype=jnp.int32))
    return total
```

```python
import functools
import math

import jax
import jax.numpy as jnp
from jax import lax
from jax.experimental import pallas as pl
from jax.experimental.pallas import tpu as pltpu
from jax.sharding import PartitionSpec as P

PANEL = 64
NX, NZ, NC, NAUX = 4, 8, 2, 4
SLABS = 2
SLOTS = 4
BLK = 64
WIDTH = SLOTS * BLK
WINDOW = 512
ROWS = 120
PAIR = NC * ROWS
TILE = 64
SHIFT = ROWS - TILE
Z_ORDER = (4, 3, 5, 2, 6, 1, 7, 0)
GROUPS = len(Z_ORDER)
X_LAG = 3
F32, BF16 = jnp.float32, jnp.bfloat16
NT = (((1,), (1,)), ((), ()))


def kernel(
    tensor, density, block_ids, counts, out,
    rows, dens, lead, weights, product, own, sibling_out, sibling_in, x_out, x_in, z_out, z_in,
    rows_sem, dens_sem, lead_sem, lead_send, lead_recv,
    c_send, c_recv, x_send, x_recv, z_send, z_recv,
):
    orb, aux = lax.axis_index("orb"), lax.axis_index("aux")
    core = lax.rem(orb, NC)
    z = lax.rem(orb // NC, NZ)
    x = orb // (NC * NZ)

    def at(x_of, z_of, core_of):
        return (x_of * NZ + z_of) * NC + core_of

    sibling = {"orb": at(x, z, 1 - core)}
    x_peer = [{"orb": at(lax.rem(x + d, NX), z, core)} for d in range(NX)]
    z_peer = [{"orb": at(x, lax.rem(z + d, NZ), core)} for d in range(NZ)]

    barrier = pltpu.get_barrier_semaphore()
    for peer in [sibling] + x_peer[1:] + z_peer[1:]:
        pl.semaphore_signal(barrier, inc=1, device_id=peer, device_id_type=pl.DeviceIdType.MESH)

    @pl.when(aux == 0)
    def _():
        for d in range(1, NAUX):
            pl.semaphore_signal(barrier, inc=1, device_id={"aux": d}, device_id_type=pl.DeviceIdType.MESH)

    @pl.when(aux != 0)
    def _():
        pl.semaphore_signal(barrier, inc=1, device_id={"aux": 0}, device_id_type=pl.DeviceIdType.MESH)

    lead_in = [
        pltpu.make_async_copy(
            tensor.at[0, 0, pl.ds(0, PANEL), :, pl.ds(128 * j, 128)], lead.at[j], lead_sem.at[j]
        )
        for j in range(2)
    ]

    @pl.when(aux == 0)
    def _():
        for copy in lead_in:
            copy.start()

    dens_in = pltpu.make_async_copy(density.at[0], dens, dens_sem)
    dens_in.start()
    rows_in = [
        [
            pltpu.make_async_copy(
                tensor.at[:, lax.rem(z + dz, NZ), :, :, pl.ds(128 * j, 128)],
                rows.at[g, j],
                rows_sem.at[g, j],
            )
            for j in range(2)
        ]
        for g, dz in enumerate(Z_ORDER)
    ]
    for pair in rows_in:
        for copy in pair:
            copy.start()

    def lead_copy(d, j):
        return pltpu.make_async_remote_copy(
            src_ref=lead.at[j], dst_ref=lead.at[j],
            send_sem=lead_send.at[d - 1, j], recv_sem=lead_recv.at[j],
            device_id={"aux": d}, device_id_type=pl.DeviceIdType.MESH,
        )

    @pl.when(aux == 0)
    def _():
        pl.semaphore_wait(barrier, 1 + NX - 1 + NZ - 1 + NAUX - 1)
        for j in range(2):
            lead_in[j].wait()
            for d in range(1, NAUX):
                lead_copy(d, j).start()

    @pl.when(aux != 0)
    def _():
        pl.semaphore_wait(barrier, 1 + NX - 1 + NZ - 1 + 1)

    dens_in.wait()
    locals_ = []

    def picks(k, shape, axis):
        column = lax.broadcasted_iota(jnp.int32, shape, axis)
        slot = column // BLK
        target = jnp.zeros(shape, jnp.int32)
        for s in range(SLOTS):
            target = jnp.where(slot == s, jnp.full(shape, block_ids[k, 0, s] * BLK), target)
        target = jnp.where(slot < jnp.full(shape, counts[0, k]), target + lax.rem(column, BLK), -1)
        window = lax.broadcasted_iota(jnp.int32, (WINDOW, WIDTH) if axis else (WIDTH, WINDOW), 1 - axis)
        return jnp.where(window == target, 1.0, 0.0).astype(BF16)

    for k in range(SLABS):
        some_rows = jnp.dot(picks(k, (WIDTH, 1), 0), dens[...], preferred_element_type=F32).astype(BF16)
        block = jnp.dot(some_rows, picks(k, (1, WIDTH), 1), preferred_element_type=F32)
        locals_.append(block.astype(BF16))

    @pl.when(aux != 0)
    def _():
        for j in range(2):
            lead_copy(1, j).wait_recv()

    leading = jnp.concatenate([lead[j].reshape(SLABS * PANEL, 128) for j in range(2)], axis=1)
    a = lax.broadcasted_iota(jnp.int32, (SLABS * PANEL, SLABS * PANEL), 0)
    b = lax.broadcasted_iota(jnp.int32, (SLABS * PANEL, SLABS * PANEL), 1)
    weight = None
    for k in range(SLABS):
        sort = jnp.where((b == SLABS * (a - k * PANEL) + k) & (a // PANEL == k), 1.0, 0.0).astype(BF16)
        chosen = jnp.dot(sort, leading, preferred_element_type=F32).astype(BF16)
        term = lax.dot_general(locals_[k], chosen, NT, preferred_element_type=F32)
        weight = term if weight is None else weight + term
    high = weight.astype(BF16)
    weights[:, : SLABS * PANEL] = high
    weights[:, SLABS * PANEL :] = (weight - high.astype(F32)).astype(BF16)

    left = lax.broadcasted_iota(jnp.int32, (TILE, 128), 1) < PANEL

    def multiply(g):
        for j in range(2):
            rows_in[g][j].wait()
        for d in range(NX):
            x_of = lax.rem(x + d, NX)
            slot_of = (g * NX + d) % 2
            strip = jnp.concatenate(
                [rows[g, j, x_of].reshape(SLABS * PAIR, 128) for j in range(2)], axis=1
            )
            y = jnp.dot(strip, weights[...], preferred_element_type=F32)
            product[slot_of] = y[:, :128] + y[:, 128:]
            for core_of, dest in ((1 - core, sibling_out), (core, own)):
                start = core_of * (SLABS * ROWS)

                def every_second(offset):
                    return product[slot_of, pl.ds(start + offset, TILE, SLABS), :]

                low = [every_second(k) for k in range(SLABS)]
                top = [every_second(SLABS * SHIFT + k) for k in range(SLABS)]
                dest[g, d] = jnp.where(left, low[0], top[1]) + pltpu.roll(
                    jnp.where(left, top[0], low[1]), PANEL, 1
                )

    def core_copy(g):
        return pltpu.make_async_remote_copy(
            src_ref=sibling_out.at[g], dst_ref=sibling_in.at[g],
            send_sem=c_send.at[g], recv_sem=c_recv.at[g],
            device_id=sibling, device_id_type=pl.DeviceIdType.MESH,
        )

    def x_copy(g, d):
        return pltpu.make_async_remote_copy(
            src_ref=x_out.at[g, d - 1], dst_ref=x_in.at[g, d - 1],
            send_sem=x_send.at[g, d - 1], recv_sem=x_recv.at[g, d - 1],
            device_id=x_peer[d], device_id_type=pl.DeviceIdType.MESH,
        )

    def z_copy(g):
        return pltpu.make_async_remote_copy(
            src_ref=z_out.at[g], dst_ref=z_in.at[g],
            send_sem=z_send.at[g], recv_sem=z_recv.at[g],
            device_id=z_peer[Z_ORDER[g]], device_id_type=pl.DeviceIdType.MESH,
        )

    def add_sibling(g):
        core_copy(g).wait_recv()
        for d in (2, 1, 3):
            x_out[g, d - 1] = (own[g, d] + sibling_in[g, d]).astype(BF16)
            x_copy(g, d).start()

    def add_x(g):
        total = own[g, 0] + sibling_in[g, 0]
        for d in (1, 3, 2):
            x_copy(g, d).wait_recv()
            total = total + x_in[g, d - 1].astype(F32)
        if g < GROUPS - 1:
            z_out[g] = total.astype(BF16)
            z_copy(g).start()
        return total

    for g in range(GROUPS):
        multiply(g)
        core_copy(g).start()
        if g >= 1:
            add_sibling(g - 1)
        if g >= X_LAG:
            add_x(g - X_LAG)
    add_sibling(GROUPS - 1)
    for g in range(GROUPS - X_LAG, GROUPS):
        total = add_x(g)
    for g in range(GROUPS - 1):
        z_copy(g).wait_recv()
        total = total + z_in[g].astype(F32)
    total = total * (1.0 / math.sqrt(SLABS * NX * NZ * NC * WIDTH))
    turned = total.T
    out[:, :TILE] = turned[:PANEL]
    out[:, TILE:] = turned[PANEL:, TILE - SHIFT :]

    for g in range(GROUPS):
        core_copy(g).wait_send()
        for d in range(1, NX):
            x_copy(g, d).wait_send()
        if g < GROUPS - 1:
            z_copy(g).wait_send()

    @pl.when(aux == 0)
    def _():
        for j in range(2):
            for d in range(1, NAUX):
                lead_copy(d, j).wait_send()


def on_device(tensor, density, block_ids, counts):
    tensor = tensor.reshape(NX, NZ, PAIR, SLABS, WIDTH)
    piece = (TILE, 128)
    return pl.pallas_call(
        kernel,
        out_shape=jax.ShapeDtypeStruct((PANEL, ROWS), F32),
        in_specs=[
            pl.BlockSpec(memory_space=pltpu.HBM),
            pl.BlockSpec(memory_space=pltpu.HBM),
            pl.BlockSpec(memory_space=pltpu.SMEM),
            pl.BlockSpec(memory_space=pltpu.SMEM),
        ],
        out_specs=pl.BlockSpec(memory_space=pltpu.VMEM),
        scratch_shapes=[
            pltpu.VMEM((GROUPS, 2, NX, PAIR, SLABS, 128), BF16),
            pltpu.VMEM((WINDOW, WINDOW), BF16),
            pltpu.VMEM((2, PANEL, SLABS, 128), BF16),
            pltpu.VMEM((WIDTH, 2 * SLABS * PANEL), BF16),
            pltpu.VMEM((2, SLABS * PAIR, 128), F32),
            pltpu.VMEM((GROUPS, NX) + piece, F32),
            pltpu.VMEM((GROUPS, NX) + piece, F32),
            pltpu.VMEM((GROUPS, NX) + piece, F32),
            pltpu.VMEM((GROUPS, NX - 1) + piece, BF16),
            pltpu.VMEM((GROUPS, NX - 1) + piece, BF16),
            pltpu.VMEM((GROUPS - 1,) + piece, BF16),
            pltpu.VMEM((GROUPS - 1,) + piece, BF16),
            pltpu.SemaphoreType.DMA((GROUPS, 2)),
            pltpu.SemaphoreType.DMA,
            pltpu.SemaphoreType.DMA((2,)),
            pltpu.SemaphoreType.DMA((NAUX - 1, 2)),
            pltpu.SemaphoreType.DMA((2,)),
            pltpu.SemaphoreType.DMA((GROUPS,)),
            pltpu.SemaphoreType.DMA((GROUPS,)),
            pltpu.SemaphoreType.DMA((GROUPS, NX - 1)),
            pltpu.SemaphoreType.DMA((GROUPS, NX - 1)),
            pltpu.SemaphoreType.DMA((GROUPS - 1,)),
            pltpu.SemaphoreType.DMA((GROUPS - 1,)),
        ],
        compiler_params=pltpu.CompilerParams(
            collective_id=0, has_side_effects=True, vmem_limit_bytes=60 << 20
        ),
    )(tensor, density, block_ids, counts.T)


def solution(mesh):
    return jax.shard_map(
        on_device,
        mesh=mesh,
        in_specs=(
            P("aux", None, "orb", None),
            P("orb", None, None),
            P(None, "orb", None),
            P(None, "orb"),
        ),
        out_specs=P(None, ("aux", "orb")),
        check_vma=False,
    )
```

```python
import functools
import math

import jax
import jax.numpy as jnp
from jax import lax
from jax.experimental import pallas as pl
from jax.experimental.pallas import tpu as pltpu
from jax.sharding import PartitionSpec as P

PANEL = 64
NX, NZ, NC, NAUX = 4, 8, 2, 4
SLABS = 2
SLOTS = 4
BLK = 64
WIDTH = SLOTS * BLK
WINDOW = 512
ROWS = 120
PAIR = NC * ROWS
TILE = 64
SHIFT = ROWS - TILE
Z_ORDER = (4, 3, 5, 2, 6, 1, 7, 0)
GROUPS = len(Z_ORDER)
C_LAG, X_LAG = 2, 8
F32, BF16 = jnp.float32, jnp.bfloat16
NT = (((1,), (1,)), ((), ()))


def kernel(
    tensor, density, block_ids_in, counts_in, out, block_ids, counts, small_sem,
    rows, dens, lead, weights, product, own, sibling_out, sibling_in, x_out, x_in, z_out, z_in,
    rows_sem, dens_sem, lead_sem, lead_send, lead_recv,
    c_send, c_recv, x_send, x_recv, z_send, z_recv,
):
    orb, aux = lax.axis_index("orb"), lax.axis_index("aux")
    core = lax.rem(orb, NC)
    z = lax.rem(orb // NC, NZ)
    x = orb // (NC * NZ)

    def at(x_of, z_of, core_of):
        return (x_of * NZ + z_of) * NC + core_of

    sibling = {"orb": at(x, z, 1 - core)}
    x_peer = [{"orb": at(lax.rem(x + d, NX), z, core)} for d in range(NX)]
    z_peer = [{"orb": at(x, lax.rem(z + d, NZ), core)} for d in range(NZ)]

    barrier = pltpu.get_barrier_semaphore()
    for peer in [sibling] + x_peer[1:] + z_peer[1:]:
        pl.semaphore_signal(barrier, inc=1, device_id=peer, device_id_type=pl.DeviceIdType.MESH)

    @pl.when(aux == 0)
    def _():
        for d in range(1, NAUX):
            pl.semaphore_signal(barrier, inc=1, device_id={"aux": d}, device_id_type=pl.DeviceIdType.MESH)

    @pl.when(aux != 0)
    def _():
        pl.semaphore_signal(barrier, inc=1, device_id={"aux": 0}, device_id_type=pl.DeviceIdType.MESH)

    lead_in = [
        pltpu.make_async_copy(
            tensor.at[0, 0, pl.ds(0, PANEL), :, pl.ds(128 * j, 128)], lead.at[j], lead_sem.at[j]
        )
        for j in range(2)
    ]

    @pl.when(aux == 0)
    def _():
        for copy in lead_in:
            copy.start()

    small_in = [
        pltpu.make_async_copy(block_ids_in, block_ids, small_sem.at[0]),
        pltpu.make_async_copy(counts_in, counts, small_sem.at[1]),
    ]
    for copy in small_in:
        copy.start()
    dens_in = pltpu.make_async_copy(density.at[0], dens, dens_sem)
    dens_in.start()
    rows_in = [
        [
            pltpu.make_async_copy(
                tensor.at[:, lax.rem(z + dz, NZ), :, :, pl.ds(128 * j, 128)],
                rows.at[g, j],
                rows_sem.at[g, j],
            )
            for j in range(2)
        ]
        for g, dz in enumerate(Z_ORDER)
    ]
    for pair in rows_in:
        for copy in pair:
            copy.start()

    def lead_copy(d, j):
        return pltpu.make_async_remote_copy(
            src_ref=lead.at[j], dst_ref=lead.at[j],
            send_sem=lead_send.at[d - 1, j], recv_sem=lead_recv.at[j],
            device_id={"aux": d}, device_id_type=pl.DeviceIdType.MESH,
        )

    @pl.when(aux == 0)
    def _():
        pl.semaphore_wait(barrier, 1 + NX - 1 + NZ - 1 + NAUX - 1)
        for j in range(2):
            lead_in[j].wait()
        for d in (3, 1, 2):
            for j in range(2):
                lead_copy(d, j).start()

    @pl.when(aux != 0)
    def _():
        pl.semaphore_wait(barrier, 1 + NX - 1 + NZ - 1 + 1)

    for copy in small_in:
        copy.wait()
    dens_in.wait()
    locals_ = []

    def picks(k, shape, axis):
        column = lax.broadcasted_iota(jnp.int32, shape, axis)
        slot = column // BLK
        target = jnp.zeros(shape, jnp.int32)
        for s in range(SLOTS):
            target = jnp.where(slot == s, jnp.full(shape, block_ids[k, 0, s] * BLK), target)
        target = jnp.where(slot < jnp.full(shape, counts[0, k]), target + lax.rem(column, BLK), -1)
        window = lax.broadcasted_iota(jnp.int32, (WINDOW, WIDTH) if axis else (WIDTH, WINDOW), 1 - axis)
        return jnp.where(window == target, 1.0, 0.0).astype(BF16)

    for k in range(SLABS):
        some_rows = jnp.dot(picks(k, (WIDTH, 1), 0), dens[...], preferred_element_type=F32).astype(BF16)
        block = jnp.dot(some_rows, picks(k, (1, WIDTH), 1), preferred_element_type=F32)
        locals_.append(block.astype(BF16))

    @pl.when(aux != 0)
    def _():
        for j in range(2):
            lead_copy(1, j).wait_recv()

    leading = jnp.concatenate([lead[j].reshape(SLABS * PANEL, 128) for j in range(2)], axis=1)
    a = lax.broadcasted_iota(jnp.int32, (SLABS * PANEL, SLABS * PANEL), 0)
    b = lax.broadcasted_iota(jnp.int32, (SLABS * PANEL, SLABS * PANEL), 1)
    weight = None
    for k in range(SLABS):
        sort = jnp.where((b == SLABS * (a - k * PANEL) + k) & (a // PANEL == k), 1.0, 0.0).astype(BF16)
        chosen = jnp.dot(sort, leading, preferred_element_type=F32).astype(BF16)
        term = lax.dot_general(locals_[k], chosen, NT, preferred_element_type=F32)
        weight = term if weight is None else weight + term
    high = weight.astype(BF16)
    weights[:, : SLABS * PANEL] = high
    weights[:, SLABS * PANEL :] = (weight - high.astype(F32)).astype(BF16)

    left = lax.broadcasted_iota(jnp.int32, (TILE, 128), 1) < PANEL

    def multiply(g):
        for j in range(2):
            rows_in[g][j].wait()
        for d in range(NX):
            x_of = lax.rem(x + d, NX)
            slot_of = (g * NX + d) % 2
            strip = jnp.concatenate(
                [rows[g, j, x_of].reshape(SLABS * PAIR, 128) for j in range(2)], axis=1
            )
            y = jnp.dot(strip, weights[...], preferred_element_type=F32)
            product[slot_of] = y[:, :128] + y[:, 128:]
            for core_of, dest in ((1 - core, sibling_out), (core, own)):
                start = core_of * (SLABS * ROWS)

                def every_second(offset):
                    return product[slot_of, pl.ds(start + offset, TILE, SLABS), :]

                low = [every_second(k) for k in range(SLABS)]
                top = [every_second(SLABS * SHIFT + k) for k in range(SLABS)]
                dest[g, d] = jnp.where(left, low[0], top[1]) + pltpu.roll(
                    jnp.where(left, top[0], low[1]), PANEL, 1
                )

    def core_copy(g):
        return pltpu.make_async_remote_copy(
            src_ref=sibling_out.at[g], dst_ref=sibling_in.at[g],
            send_sem=c_send.at[g], recv_sem=c_recv.at[g],
            device_id=sibling, device_id_type=pl.DeviceIdType.MESH,
        )

    def x_copy(g, d):
        return pltpu.make_async_remote_copy(
            src_ref=x_out.at[g, d - 1], dst_ref=x_in.at[g, d - 1],
            send_sem=x_send.at[g, d - 1], recv_sem=x_recv.at[g, d - 1],
            device_id=x_peer[d], device_id_type=pl.DeviceIdType.MESH,
        )

    def z_copy(g):
        return pltpu.make_async_remote_copy(
            src_ref=z_out.at[g], dst_ref=z_in.at[g],
            send_sem=z_send.at[g], recv_sem=z_recv.at[g],
            device_id=z_peer[Z_ORDER[g]], device_id_type=pl.DeviceIdType.MESH,
        )

    def add_sibling(g):
        core_copy(g).wait_recv()
        for d in (2, 1, 3):
            x_out[g, d - 1] = (own[g, d] + sibling_in[g, d]).astype(BF16)
            x_copy(g, d).start()

    def add_x(g):
        total = own[g, 0] + sibling_in[g, 0]
        for d in (1, 3, 2):
            x_copy(g, d).wait_recv()
            total = total + x_in[g, d - 1].astype(F32)
        if g < GROUPS - 1:
            z_out[g] = total.astype(BF16)
            z_copy(g).start()
        return total

    for g in range(GROUPS):
        multiply(g)
        core_copy(g).start()
        if g >= C_LAG:
            add_sibling(g - C_LAG)
        if g >= X_LAG:
            add_x(g - X_LAG)
    for g in range(GROUPS - C_LAG, GROUPS):
        add_sibling(g)
    for g in range(GROUPS - X_LAG, GROUPS):
        total = add_x(g)
    for g in range(GROUPS - 1):
        z_copy(g).wait_recv()
        total = total + z_in[g].astype(F32)
    total = total * (1.0 / math.sqrt(SLABS * NX * NZ * NC * WIDTH))
    turned = total.T
    out[:, :TILE] = turned[:PANEL]
    out[:, TILE:] = turned[PANEL:, TILE - SHIFT :]

    for g in range(GROUPS):
        core_copy(g).wait_send()
        for d in range(1, NX):
            x_copy(g, d).wait_send()
        if g < GROUPS - 1:
            z_copy(g).wait_send()

    @pl.when(aux == 0)
    def _():
        for j in range(2):
            for d in range(1, NAUX):
                lead_copy(d, j).wait_send()


def on_device(tensor, density, block_ids, counts):
    tensor = tensor.reshape(NX, NZ, PAIR, SLABS, WIDTH)
    piece = (TILE, 128)
    return pl.pallas_call(
        kernel,
        out_shape=jax.ShapeDtypeStruct((PANEL, ROWS), F32),
        in_specs=[
            pl.BlockSpec(memory_space=pltpu.HBM),
            pl.BlockSpec(memory_space=pltpu.HBM),
            pl.BlockSpec(memory_space=pltpu.HBM),
            pl.BlockSpec(memory_space=pltpu.HBM),
        ],
        out_specs=pl.BlockSpec(memory_space=pltpu.VMEM),
        scratch_shapes=[
            pltpu.SMEM((SLABS, 1, SLOTS), jnp.int32),
            pltpu.SMEM((1, SLABS), jnp.int32),
            pltpu.SemaphoreType.DMA((2,)),
            pltpu.VMEM((GROUPS, 2, NX, PAIR, SLABS, 128), BF16),
            pltpu.VMEM((WINDOW, WINDOW), BF16),
            pltpu.VMEM((2, PANEL, SLABS, 128), BF16),
            pltpu.VMEM((WIDTH, 2 * SLABS * PANEL), BF16),
            pltpu.VMEM((2, SLABS * PAIR, 128), F32),
            pltpu.VMEM((GROUPS, NX) + piece, F32),
            pltpu.VMEM((GROUPS, NX) + piece, F32),
            pltpu.VMEM((GROUPS, NX) + piece, F32),
            pltpu.VMEM((GROUPS, NX - 1) + piece, BF16),
            pltpu.VMEM((GROUPS, NX - 1) + piece, BF16),
            pltpu.VMEM((GROUPS - 1,) + piece, BF16),
            pltpu.VMEM((GROUPS - 1,) + piece, BF16),
            pltpu.SemaphoreType.DMA((GROUPS, 2)),
            pltpu.SemaphoreType.DMA,
            pltpu.SemaphoreType.DMA((2,)),
            pltpu.SemaphoreType.DMA((NAUX - 1, 2)),
            pltpu.SemaphoreType.DMA((2,)),
            pltpu.SemaphoreType.DMA((GROUPS,)),
            pltpu.SemaphoreType.DMA((GROUPS,)),
            pltpu.SemaphoreType.DMA((GROUPS, NX - 1)),
            pltpu.SemaphoreType.DMA((GROUPS, NX - 1)),
            pltpu.SemaphoreType.DMA((GROUPS - 1,)),
            pltpu.SemaphoreType.DMA((GROUPS - 1,)),
        ],
        compiler_params=pltpu.CompilerParams(
            collective_id=0, has_side_effects=True, vmem_limit_bytes=32 << 20
        ),
    )(*[pltpu.with_memory_space_constraint(a, pltpu.HBM) for a in (tensor, density, block_ids, counts.T)])


def solution(mesh):
    return jax.shard_map(
        on_device,
        mesh=mesh,
        in_specs=(
            P("aux", None, "orb", None),
            P("orb", None, None),
            P(None, "orb", None),
            P(None, "orb"),
        ),
        out_specs=P(None, ("aux", "orb")),
        check_vma=False,
    )
```

```python
import functools
import math

import jax
import jax.numpy as jnp
from jax import lax
from jax.experimental import pallas as pl
from jax.experimental.pallas import tpu as pltpu
from jax.sharding import PartitionSpec as P

PANEL = 64
NX, NZ, NC, NAUX = 4, 8, 2, 4
SLABS = 2
SLOTS = 4
BLK = 64
WIDTH = SLOTS * BLK
WINDOW = 512
ROWS = 120
PAIR = NC * ROWS
TILE = 64
SHIFT = ROWS - TILE
GROUPS = NZ
BLOCKS = ((0,), (1,), (2,), (3,), (4,), (5,), (6,), (7,))
C_LAG, X_LAG = 2, 4
F32, BF16 = jnp.float32, jnp.bfloat16
NT = (((1,), (1,)), ((), ()))


def kernel(
    tensor, density, block_ids_in, counts_in, out, block_ids, counts, small_sem,
    rows, dens, lead, weights, product, own, sibling_out, sibling_in, x_out, x_in, totals, z_out, z_in,
    rows_sem, dens_sem, lead_sem, lead_send, lead_recv,
    z_ready, c_send, c_recv, x_send, x_recv, z_send, z_recv,
):
    orb, aux = lax.axis_index("orb"), lax.axis_index("aux")
    core = lax.rem(orb, NC)
    z = lax.rem(orb // NC, NZ)
    x = orb // (NC * NZ)

    def at(x_of, z_of, core_of):
        return (x_of * NZ + z_of) * NC + core_of

    sibling = {"orb": at(x, z, 1 - core)}
    x_peer = [{"orb": at(lax.rem(x + d, NX), z, core)} for d in range(NX)]
    z_peer = [{"orb": at(x, of, core)} for of in range(NZ)]

    barrier = pltpu.get_barrier_semaphore()
    for peer in [sibling] + x_peer[1:]:
        pl.semaphore_signal(barrier, inc=1, device_id=peer, device_id_type=pl.DeviceIdType.MESH)
    for of in range(1, NZ):
        @pl.when(z < of)
        def _():
            pl.semaphore_signal(barrier, inc=1, device_id=z_peer[of], device_id_type=pl.DeviceIdType.MESH)

    @pl.when(aux == 0)
    def _():
        for d in range(1, NAUX):
            pl.semaphore_signal(barrier, inc=1, device_id={"aux": d}, device_id_type=pl.DeviceIdType.MESH)

    @pl.when(aux != 0)
    def _():
        pl.semaphore_signal(barrier, inc=1, device_id={"aux": 0}, device_id_type=pl.DeviceIdType.MESH)

    lead_in = [
        pltpu.make_async_copy(
            tensor.at[0, 0, pl.ds(0, PANEL), :, pl.ds(128 * j, 128)], lead.at[j], lead_sem.at[j]
        )
        for j in range(2)
    ]

    @pl.when(aux == 0)
    def _():
        for copy in lead_in:
            copy.start()

    small_in = [
        pltpu.make_async_copy(block_ids_in, block_ids, small_sem.at[0]),
        pltpu.make_async_copy(counts_in, counts, small_sem.at[1]),
    ]
    for copy in small_in:
        copy.start()
    dens_in = pltpu.make_async_copy(density.at[0], dens, dens_sem)
    dens_in.start()
    rows_in = [
        [
            pltpu.make_async_copy(
                tensor.at[:, g, :, :, pl.ds(128 * j, 128)],
                rows.at[g, j],
                rows_sem.at[g, j],
            )
            for j in range(2)
        ]
        for g in range(GROUPS)
    ]
    for pair in rows_in:
        for copy in pair:
            copy.start()

    def lead_copy(d, j):
        return pltpu.make_async_remote_copy(
            src_ref=lead.at[j], dst_ref=lead.at[j],
            send_sem=lead_send.at[d - 1, j], recv_sem=lead_recv.at[j],
            device_id={"aux": d}, device_id_type=pl.DeviceIdType.MESH,
        )

    @pl.when(aux == 0)
    def _():
        pl.semaphore_wait(barrier, 1 + NX - 1 + NAUX - 1 + z)
        for j in range(2):
            lead_in[j].wait()
        for d in (2, 1, 3):
            for j in range(2):
                lead_copy(d, j).start()

    @pl.when(aux != 0)
    def _():
        pl.semaphore_wait(barrier, 1 + NX - 1 + 1 + z)

    for of in range(NZ - 1):
        @pl.when(z > of)
        def _():
            pl.semaphore_signal(z_ready.at[z], inc=1, device_id=z_peer[of], device_id_type=pl.DeviceIdType.MESH)

    for copy in small_in:
        copy.wait()
    dens_in.wait()
    locals_ = []

    def picks(k, shape, axis):
        column = lax.broadcasted_iota(jnp.int32, shape, axis)
        slot = column // BLK
        target = jnp.zeros(shape, jnp.int32)
        for s in range(SLOTS):
            target = jnp.where(slot == s, jnp.full(shape, block_ids[k, 0, s] * BLK), target)
        target = jnp.where(slot < jnp.full(shape, counts[0, k]), target + lax.rem(column, BLK), -1)
        window = lax.broadcasted_iota(jnp.int32, (WINDOW, WIDTH) if axis else (WIDTH, WINDOW), 1 - axis)
        return jnp.where(window == target, 1.0, 0.0).astype(BF16)

    for k in range(SLABS):
        some_rows = jnp.dot(picks(k, (WIDTH, 1), 0), dens[...], preferred_element_type=F32).astype(BF16)
        block = jnp.dot(some_rows, picks(k, (1, WIDTH), 1), preferred_element_type=F32)
        locals_.append(block.astype(BF16))

    @pl.when(aux != 0)
    def _():
        for j in range(2):
            lead_copy(1, j).wait_recv()

    leading = jnp.concatenate([lead[j].reshape(SLABS * PANEL, 128) for j in range(2)], axis=1)
    a = lax.broadcasted_iota(jnp.int32, (SLABS * PANEL, SLABS * PANEL), 0)
    b = lax.broadcasted_iota(jnp.int32, (SLABS * PANEL, SLABS * PANEL), 1)
    weight = None
    for k in range(SLABS):
        sort = jnp.where((b == SLABS * (a - k * PANEL) + k) & (a // PANEL == k), 1.0, 0.0).astype(BF16)
        chosen = jnp.dot(sort, leading, preferred_element_type=F32).astype(BF16)
        term = lax.dot_general(locals_[k], chosen, NT, preferred_element_type=F32)
        weight = term if weight is None else weight + term
    high = weight.astype(BF16)
    weights[:, : SLABS * PANEL] = high
    weights[:, SLABS * PANEL :] = (weight - high.astype(F32)).astype(BF16)

    left = lax.broadcasted_iota(jnp.int32, (TILE, 128), 1) < PANEL

    def multiply(g):
        for d in range(NX):
            x_of = lax.rem(x + d, NX)
            slot_of = (g * NX + d) % 4
            strip = jnp.concatenate(
                [rows[g, j, x_of].reshape(SLABS * PAIR, 128) for j in range(2)], axis=1
            )
            y = jnp.dot(strip, weights[...], preferred_element_type=F32)
            product[slot_of] = y[:, :128] + y[:, 128:]
            for core_of, dest in ((1 - core, sibling_out), (core, own)):
                start = core_of * (SLABS * ROWS)

                def every_second(offset):
                    return product[slot_of, pl.ds(start + offset, TILE, SLABS), :]

                low = [every_second(k) for k in range(SLABS)]
                top = [every_second(SLABS * SHIFT + k) for k in range(SLABS)]
                dest[g, d] = jnp.where(left, low[0], top[1]) + pltpu.roll(
                    jnp.where(left, top[0], low[1]), PANEL, 1
                )

    def core_copy(g):
        return pltpu.make_async_remote_copy(
            src_ref=sibling_out.at[g], dst_ref=sibling_in.at[g],
            send_sem=c_send.at[g], recv_sem=c_recv.at[g],
            device_id=sibling, device_id_type=pl.DeviceIdType.MESH,
        )

    def x_copy(g, d):
        return pltpu.make_async_remote_copy(
            src_ref=x_out.at[g, d - 1], dst_ref=x_in.at[g, d - 1],
            send_sem=x_send.at[g, d - 1], recv_sem=x_recv.at[g, d - 1],
            device_id=x_peer[d], device_id_type=pl.DeviceIdType.MESH,
        )

    def z_copy(g, slot):
        return pltpu.make_async_remote_copy(
            src_ref=z_out.at[g], dst_ref=z_in.at[slot],
            send_sem=z_send.at[g], recv_sem=z_recv.at[slot],
            device_id={"orb": at(x, g, core)}, device_id_type=pl.DeviceIdType.MESH,
        )

    def z_slot(g):
        return lax.rem(z - g + 2 * NZ - 1, NZ)

    def add_sibling(g):
        for d in range(1, NX):
            x_out[g, d - 1] = (own[g, d] + sibling_in[g, d]).astype(BF16)

    def add_x(g):
        total = own[g, 0] + sibling_in[g, 0]
        for d in (1, 3, 2):
            x_copy(g, d).wait_recv()
            total = total + x_in[g, d - 1].astype(F32)
        totals[g] = total
        z_out[g] = total.astype(BF16)

        @pl.when(z < g)
        def _():
            pl.semaphore_wait(z_ready.at[g], 1)

        @pl.when(z != g)
        def _():
            z_copy(g, z_slot(g)).start()

    for pair in rows_in:
        for copy in pair:
            copy.wait()
    for step in range(len(BLOCKS) + C_LAG + X_LAG):
        fresh = BLOCKS[step] if step < len(BLOCKS) else ()
        ripe = BLOCKS[step - C_LAG] if 0 <= step - C_LAG < len(BLOCKS) else ()
        done = BLOCKS[step - C_LAG - X_LAG] if step >= C_LAG + X_LAG else ()
        for g in ripe:
            core_copy(g).wait_recv()
        for g in ripe:
            add_sibling(g)
        if not fresh:
            for g in ripe:
                for d in (2, 1, 3):
                    x_copy(g, d).start()
        for g in fresh:
            multiply(g)
        if fresh:
            for g in ripe:
                for d in (2, 1, 3):
                    x_copy(g, d).start()
        for g in fresh:
            core_copy(g).start()
        for g in done:
            add_x(g)
    total = totals[z]
    for slot in range(NZ - 1):
        z_copy(0, slot).wait_recv()
        total = total + z_in[slot].astype(F32)
    total = total * (1.0 / math.sqrt(SLABS * NX * NZ * NC * WIDTH))
    turned = total.T
    out[:, :TILE] = turned[:PANEL]
    out[:, TILE:] = turned[PANEL:, TILE - SHIFT :]

    for g in range(GROUPS):
        core_copy(g).wait_send()
        for d in range(1, NX):
            x_copy(g, d).wait_send()

        @pl.when(z != g)
        def _():
            z_copy(g, z_slot(g)).wait_send()

    @pl.when(aux == 0)
    def _():
        for j in range(2):
            for d in range(1, NAUX):
                lead_copy(d, j).wait_send()


def on_device(tensor, density, block_ids, counts):
    tensor = tensor.reshape(NX, NZ, PAIR, SLABS, WIDTH)
    piece = (TILE, 128)
    return pl.pallas_call(
        kernel,
        out_shape=jax.ShapeDtypeStruct((PANEL, ROWS), F32),
        in_specs=[
            pl.BlockSpec(memory_space=pltpu.HBM),
            pl.BlockSpec(memory_space=pltpu.HBM),
            pl.BlockSpec(memory_space=pltpu.HBM),
            pl.BlockSpec(memory_space=pltpu.HBM),
        ],
        out_specs=pl.BlockSpec(memory_space=pltpu.VMEM),
        scratch_shapes=[
            pltpu.SMEM((SLABS, 1, SLOTS), jnp.int32),
            pltpu.SMEM((1, SLABS), jnp.int32),
            pltpu.SemaphoreType.DMA((2,)),
            pltpu.VMEM((GROUPS, 2, NX, PAIR, SLABS, 128), BF16),
            pltpu.VMEM((WINDOW, WINDOW), BF16),
            pltpu.VMEM((2, PANEL, SLABS, 128), BF16),
            pltpu.VMEM((WIDTH, 2 * SLABS * PANEL), BF16),
            pltpu.VMEM((4, SLABS * PAIR, 128), F32),
            pltpu.VMEM((GROUPS, NX) + piece, F32),
            pltpu.VMEM((GROUPS, NX) + piece, F32),
            pltpu.VMEM((GROUPS, NX) + piece, F32),
            pltpu.VMEM((GROUPS, NX - 1) + piece, BF16),
            pltpu.VMEM((GROUPS, NX - 1) + piece, BF16),
            pltpu.VMEM((GROUPS,) + piece, F32),
            pltpu.VMEM((GROUPS,) + piece, BF16),
            pltpu.VMEM((NZ,) + piece, BF16),
            pltpu.SemaphoreType.DMA((GROUPS, 2)),
            pltpu.SemaphoreType.DMA,
            pltpu.SemaphoreType.DMA((2,)),
            pltpu.SemaphoreType.DMA((NAUX - 1, 2)),
            pltpu.SemaphoreType.DMA((2,)),
            pltpu.SemaphoreType.REGULAR((NZ,)),
            pltpu.SemaphoreType.DMA((GROUPS,)),
            pltpu.SemaphoreType.DMA((GROUPS,)),
            pltpu.SemaphoreType.DMA((GROUPS, NX - 1)),
            pltpu.SemaphoreType.DMA((GROUPS, NX - 1)),
            pltpu.SemaphoreType.DMA((GROUPS,)),
            pltpu.SemaphoreType.DMA((NZ,)),
        ],
        compiler_params=pltpu.CompilerParams(
            collective_id=0, has_side_effects=True, vmem_limit_bytes=32 << 20
        ),
    )(*[pltpu.with_memory_space_constraint(a, pltpu.HBM) for a in (tensor, density, block_ids, counts.T)])


def solution(mesh):
    return jax.shard_map(
        on_device,
        mesh=mesh,
        in_specs=(
            P("aux", None, "orb", None),
            P("orb", None, None),
            P(None, "orb", None),
            P(None, "orb"),
        ),
        out_specs=P(None, ("aux", "orb")),
        check_vma=False,
    )
```

```python
import functools
import math

import jax
import jax.numpy as jnp
from jax import lax
from jax.experimental import pallas as pl
from jax.experimental.pallas import tpu as pltpu
from jax.sharding import PartitionSpec as P

PANEL = 64
NX, NZ, NC, NAUX = 4, 8, 2, 4
SLABS = 2
SLOTS = 4
BLK = 64
WIDTH = SLOTS * BLK
WINDOW = 512
ROWS = 120
PAIR = NC * ROWS
TILE = 64
SHIFT = ROWS - TILE
GROUPS = NZ
BLOCKS = ((0,), (1,), (2,), (3,), (4,), (5,), (6,), (7,))
C_LAG, X_LAG = 2, 4
F32, BF16 = jnp.float32, jnp.bfloat16
NT = (((1,), (1,)), ((), ()))


def kernel(
    tensor, density, block_ids_in, counts_in, out, block_ids, counts, small_sem,
    rows, dens, lead, weights, product, own, sibling_out, sibling_in, x_out, x_in, totals, z_out, z_in,
    rows_sem, dens_sem, lead_sem, lead_send, lead_recv,
    z_ready, c_send, c_recv, x_send, x_recv, z_send, z_recv,
):
    orb, aux = lax.axis_index("orb"), lax.axis_index("aux")
    core = lax.rem(orb, NC)
    z = lax.rem(orb // NC, NZ)
    x = orb // (NC * NZ)

    def at(x_of, z_of, core_of):
        return (x_of * NZ + z_of) * NC + core_of

    sibling = {"orb": at(x, z, 1 - core)}
    x_peer = [{"orb": at(lax.rem(x + d, NX), z, core)} for d in range(NX)]
    z_peer = [{"orb": at(x, of, core)} for of in range(NZ)]

    barrier = pltpu.get_barrier_semaphore()

    @pl.when(aux == 0)
    def _():
        for d in range(1, NAUX):
            pl.semaphore_signal(barrier, inc=1, device_id={"aux": d}, device_id_type=pl.DeviceIdType.MESH)

    @pl.when(aux != 0)
    def _():
        pl.semaphore_signal(barrier, inc=1, device_id={"aux": 0}, device_id_type=pl.DeviceIdType.MESH)

    for peer in [sibling] + x_peer[1:]:
        pl.semaphore_signal(barrier, inc=1, device_id=peer, device_id_type=pl.DeviceIdType.MESH)
    for of in range(1, NZ):
        @pl.when(z < of)
        def _():
            pl.semaphore_signal(barrier, inc=1, device_id=z_peer[of], device_id_type=pl.DeviceIdType.MESH)

    lead_in = [
        pltpu.make_async_copy(
            tensor.at[0, 0, pl.ds(0, PANEL), :, pl.ds(128 * j, 128)], lead.at[j], lead_sem.at[j]
        )
        for j in range(2)
    ]

    @pl.when(aux == 0)
    def _():
        for copy in lead_in:
            copy.start()

    small_in = [
        pltpu.make_async_copy(block_ids_in, block_ids, small_sem.at[0]),
        pltpu.make_async_copy(counts_in, counts, small_sem.at[1]),
    ]
    for copy in small_in:
        copy.start()
    dens_in = pltpu.make_async_copy(density.at[0], dens, dens_sem)
    dens_in.start()
    rows_in = [
        [
            pltpu.make_async_copy(
                tensor.at[:, g, :, :, pl.ds(128 * j, 128)],
                rows.at[g, j],
                rows_sem.at[g, j],
            )
            for j in range(2)
        ]
        for g in range(GROUPS)
    ]
    for pair in rows_in:
        for copy in pair:
            copy.start()

    def lead_copy(d, j):
        return pltpu.make_async_remote_copy(
            src_ref=lead.at[j], dst_ref=lead.at[j],
            send_sem=lead_send.at[d - 1, j], recv_sem=lead_recv.at[j],
            device_id={"aux": d}, device_id_type=pl.DeviceIdType.MESH,
        )

    @pl.when(aux == 0)
    def _():
        pl.semaphore_wait(barrier, 1 + NX - 1 + NAUX - 1 + z)
        for j in range(2):
            lead_in[j].wait()
        for j in range(2):
            for d in (1, 2, 3):
                lead_copy(d, j).start()

    @pl.when(aux != 0)
    def _():
        pl.semaphore_wait(barrier, 1 + NX - 1 + 1 + z)

    for of in range(NZ - 1):
        @pl.when(z > of)
        def _():
            pl.semaphore_signal(z_ready.at[z], inc=1, device_id=z_peer[of], device_id_type=pl.DeviceIdType.MESH)

    for copy in small_in:
        copy.wait()
    dens_in.wait()
    locals_ = []

    def picks(k, shape, axis):
        column = lax.broadcasted_iota(jnp.int32, shape, axis)
        slot = column // BLK
        target = jnp.zeros(shape, jnp.int32)
        for s in range(SLOTS):
            target = jnp.where(slot == s, jnp.full(shape, block_ids[k, 0, s] * BLK), target)
        target = jnp.where(slot < jnp.full(shape, counts[0, k]), target + lax.rem(column, BLK), -1)
        window = lax.broadcasted_iota(jnp.int32, (WINDOW, WIDTH) if axis else (WIDTH, WINDOW), 1 - axis)
        return jnp.where(window == target, 1.0, 0.0).astype(BF16)

    for k in range(SLABS):
        some_rows = jnp.dot(picks(k, (WIDTH, 1), 0), dens[...], preferred_element_type=F32).astype(BF16)
        block = jnp.dot(some_rows, picks(k, (1, WIDTH), 1), preferred_element_type=F32)
        locals_.append(block.astype(BF16))

    @pl.when(aux != 0)
    def _():
        for j in range(2):
            lead_copy(1, j).wait_recv()

    leading = jnp.concatenate([lead[j].reshape(SLABS * PANEL, 128) for j in range(2)], axis=1)
    a = lax.broadcasted_iota(jnp.int32, (SLABS * PANEL, SLABS * PANEL), 0)
    b = lax.broadcasted_iota(jnp.int32, (SLABS * PANEL, SLABS * PANEL), 1)
    weight = None
    for k in range(SLABS):
        sort = jnp.where((b == SLABS * (a - k * PANEL) + k) & (a // PANEL == k), 1.0, 0.0).astype(BF16)
        chosen = jnp.dot(sort, leading, preferred_element_type=F32).astype(BF16)
        term = lax.dot_general(locals_[k], chosen, NT, preferred_element_type=F32)
        weight = term if weight is None else weight + term
    high = weight.astype(BF16)
    weights[:, : SLABS * PANEL] = high
    weights[:, SLABS * PANEL :] = (weight - high.astype(F32)).astype(BF16)

    left = lax.broadcasted_iota(jnp.int32, (TILE, 128), 1) < PANEL

    def multiply(g):
        for d in range(NX):
            x_of = lax.rem(x + d, NX)
            slot_of = (g * NX + d) % 4
            strip = jnp.concatenate(
                [rows[g, j, x_of].reshape(SLABS * PAIR, 128) for j in range(2)], axis=1
            )
            y = jnp.dot(strip, weights[...], preferred_element_type=F32)
            product[slot_of] = y[:, :128] + y[:, 128:]
            for core_of, dest in ((1 - core, sibling_out), (core, own)):
                start = core_of * (SLABS * ROWS)

                def every_second(offset):
                    return product[slot_of, pl.ds(start + offset, TILE, SLABS), :]

                low = [every_second(k) for k in range(SLABS)]
                top = [every_second(SLABS * SHIFT + k) for k in range(SLABS)]
                dest[g, d] = jnp.where(left, low[0], top[1]) + pltpu.roll(
                    jnp.where(left, top[0], low[1]), PANEL, 1
                )

    def core_copy(g):
        return pltpu.make_async_remote_copy(
            src_ref=sibling_out.at[g], dst_ref=sibling_in.at[g],
            send_sem=c_send.at[g], recv_sem=c_recv.at[g],
            device_id=sibling, device_id_type=pl.DeviceIdType.MESH,
        )

    def x_copy(g, d):
        return pltpu.make_async_remote_copy(
            src_ref=x_out.at[g, d - 1], dst_ref=x_in.at[g, d - 1],
            send_sem=x_send.at[g, d - 1], recv_sem=x_recv.at[g, d - 1],
            device_id=x_peer[d], device_id_type=pl.DeviceIdType.MESH,
        )

    def z_copy(g, slot):
        return pltpu.make_async_remote_copy(
            src_ref=z_out.at[g], dst_ref=z_in.at[slot],
            send_sem=z_send.at[g], recv_sem=z_recv.at[slot],
            device_id={"orb": at(x, g, core)}, device_id_type=pl.DeviceIdType.MESH,
        )

    def z_slot(g):
        return lax.rem(z - g + 2 * NZ - 1, NZ)

    def add_sibling(g):
        for d in range(1, NX):
            x_out[g, d - 1] = (own[g, d] + sibling_in[g, d]).astype(BF16)

    def add_x(g):
        total = own[g, 0] + sibling_in[g, 0]
        for d in (1, 3, 2):
            x_copy(g, d).wait_recv()
            total = total + x_in[g, d - 1].astype(F32)
        totals[g] = total
        z_out[g] = total.astype(BF16)

        @pl.when(z < g)
        def _():
            pl.semaphore_wait(z_ready.at[g], 1)

        @pl.when(z != g)
        def _():
            z_copy(g, z_slot(g)).start()

    for pair in rows_in:
        for copy in pair:
            copy.wait()
    for step in range(len(BLOCKS) + C_LAG + X_LAG):
        fresh = BLOCKS[step] if step < len(BLOCKS) else ()
        ripe = BLOCKS[step - C_LAG] if 0 <= step - C_LAG < len(BLOCKS) else ()
        done = BLOCKS[step - C_LAG - X_LAG] if step >= C_LAG + X_LAG else ()
        for g in ripe:
            core_copy(g).wait_recv()
        for g in ripe:
            add_sibling(g)
        if not fresh:
            for g in ripe:
                for d in (2, 1, 3):
                    x_copy(g, d).start()
        for g in fresh:
            multiply(g)
        if fresh:
            for g in ripe:
                for d in (2, 1, 3):
                    x_copy(g, d).start()
        for g in fresh:
            core_copy(g).start()
        for g in done:
            add_x(g)
    total = totals[z]
    for slot in range(NZ - 1):
        z_copy(0, slot).wait_recv()
        total = total + z_in[slot].astype(F32)
    total = total * (1.0 / math.sqrt(SLABS * NX * NZ * NC * WIDTH))
    turned = total.T
    out[:, :TILE] = turned[:PANEL]
    out[:, TILE:] = turned[PANEL:, TILE - SHIFT :]

    for g in range(GROUPS):
        core_copy(g).wait_send()
        for d in range(1, NX):
            x_copy(g, d).wait_send()

        @pl.when(z != g)
        def _():
            z_copy(g, z_slot(g)).wait_send()

    @pl.when(aux == 0)
    def _():
        for j in range(2):
            for d in range(1, NAUX):
                lead_copy(d, j).wait_send()


def on_device(tensor, density, block_ids, counts):
    tensor = tensor.reshape(NX, NZ, PAIR, SLABS, WIDTH)
    piece = (TILE, 128)
    return pl.pallas_call(
        kernel,
        out_shape=jax.ShapeDtypeStruct((PANEL, ROWS), F32),
        in_specs=[
            pl.BlockSpec(memory_space=pltpu.HBM),
            pl.BlockSpec(memory_space=pltpu.HBM),
            pl.BlockSpec(memory_space=pltpu.HBM),
            pl.BlockSpec(memory_space=pltpu.HBM),
        ],
        out_specs=pl.BlockSpec(memory_space=pltpu.VMEM),
        scratch_shapes=[
            pltpu.SMEM((SLABS, 1, SLOTS), jnp.int32),
            pltpu.SMEM((1, SLABS), jnp.int32),
            pltpu.SemaphoreType.DMA((2,)),
            pltpu.VMEM((GROUPS, 2, NX, PAIR, SLABS, 128), BF16),
            pltpu.VMEM((WINDOW, WINDOW), BF16),
            pltpu.VMEM((2, PANEL, SLABS, 128), BF16),
            pltpu.VMEM((WIDTH, 2 * SLABS * PANEL), BF16),
            pltpu.VMEM((4, SLABS * PAIR, 128), F32),
            pltpu.VMEM((GROUPS, NX) + piece, F32),
            pltpu.VMEM((GROUPS, NX) + piece, F32),
            pltpu.VMEM((GROUPS, NX) + piece, F32),
            pltpu.VMEM((GROUPS, NX - 1) + piece, BF16),
            pltpu.VMEM((GROUPS, NX - 1) + piece, BF16),
            pltpu.VMEM((GROUPS,) + piece, F32),
            pltpu.VMEM((GROUPS,) + piece, BF16),
            pltpu.VMEM((NZ,) + piece, BF16),
            pltpu.SemaphoreType.DMA((GROUPS, 2)),
            pltpu.SemaphoreType.DMA,
            pltpu.SemaphoreType.DMA((2,)),
            pltpu.SemaphoreType.DMA((NAUX - 1, 2)),
            pltpu.SemaphoreType.DMA((2,)),
            pltpu.SemaphoreType.REGULAR((NZ,)),
            pltpu.SemaphoreType.DMA((GROUPS,)),
            pltpu.SemaphoreType.DMA((GROUPS,)),
            pltpu.SemaphoreType.DMA((GROUPS, NX - 1)),
            pltpu.SemaphoreType.DMA((GROUPS, NX - 1)),
            pltpu.SemaphoreType.DMA((GROUPS,)),
            pltpu.SemaphoreType.DMA((NZ,)),
        ],
        compiler_params=pltpu.CompilerParams(
            collective_id=0, has_side_effects=True, vmem_limit_bytes=32 << 20
        ),
    )(*[pltpu.with_memory_space_constraint(a, pltpu.HBM) for a in (tensor, density, block_ids, counts.T)])


def solution(mesh):
    return jax.shard_map(
        on_device,
        mesh=mesh,
        in_specs=(
            P("aux", None, "orb", None),
            P("orb", None, None),
            P(None, "orb", None),
            P(None, "orb"),
        ),
        out_specs=P(None, ("aux", "orb")),
        check_vma=False,
    )
```

```python
import functools
import math

import jax
import jax.numpy as jnp
from jax import lax
from jax.experimental import pallas as pl
from jax.experimental.pallas import tpu as pltpu
from jax.sharding import PartitionSpec as P

PANEL = 64
NX, NZ, NC, NAUX = 4, 8, 2, 4
SLABS = 2
SLOTS = 4
BLK = 64
WIDTH = SLOTS * BLK
WINDOW = 512
ROWS = 120
PAIR = NC * ROWS
TILE = 64
SHIFT = ROWS - TILE
GROUPS = NZ
BLOCKS = ((0,), (1,), (2,), (3,), (4,), (5,), (6,), (7,))
C_LAG, X_LAG = 2, 4
F32, BF16 = jnp.float32, jnp.bfloat16
NT = (((1,), (1,)), ((), ()))


def kernel(
    tensor, density, block_ids_in, counts_in, out, block_ids, counts, small_sem,
    rows, dens, lead, weights, product, own, sibling_out, sibling_in, x_out, x_in, totals, z_out, z_in,
    rows_sem, dens_sem, lead_sem, lead_send, lead_recv,
    z_ready, c_send, c_recv, x_send, x_recv, z_send, z_recv,
):
    orb, aux = lax.axis_index("orb"), lax.axis_index("aux")
    core = lax.rem(orb, NC)
    z = lax.rem(orb // NC, NZ)
    x = orb // (NC * NZ)

    def at(x_of, z_of, core_of):
        return (x_of * NZ + z_of) * NC + core_of

    sibling = {"orb": at(x, z, 1 - core)}
    x_peer = [{"orb": at(lax.rem(x + d, NX), z, core)} for d in range(NX)]
    z_peer = [{"orb": at(x, of, core)} for of in range(NZ)]

    barrier = pltpu.get_barrier_semaphore()

    @pl.when(aux == 0)
    def _():
        for d in range(1, NAUX):
            pl.semaphore_signal(barrier, inc=1, device_id={"aux": d}, device_id_type=pl.DeviceIdType.MESH)

    @pl.when(aux != 0)
    def _():
        pl.semaphore_signal(barrier, inc=1, device_id={"aux": 0}, device_id_type=pl.DeviceIdType.MESH)

    for peer in [sibling] + x_peer[1:]:
        pl.semaphore_signal(barrier, inc=1, device_id=peer, device_id_type=pl.DeviceIdType.MESH)
    for of in range(1, NZ):
        @pl.when(z < of)
        def _():
            pl.semaphore_signal(barrier, inc=1, device_id=z_peer[of], device_id_type=pl.DeviceIdType.MESH)

    lead_in = [
        pltpu.make_async_copy(
            tensor.at[0, 0, pl.ds(0, PANEL), :, pl.ds(128 * j, 128)], lead.at[j], lead_sem.at[j]
        )
        for j in range(2)
    ]

    @pl.when(aux == 0)
    def _():
        for copy in lead_in:
            copy.start()

    small_in = [
        pltpu.make_async_copy(block_ids_in, block_ids, small_sem.at[0]),
        pltpu.make_async_copy(counts_in, counts, small_sem.at[1]),
    ]
    for copy in small_in:
        copy.start()
    dens_in = pltpu.make_async_copy(density.at[0], dens, dens_sem)
    dens_in.start()
    rows_in = [
        [
            pltpu.make_async_copy(
                tensor.at[:, g, :, :, pl.ds(128 * j, 128)],
                rows.at[g, j],
                rows_sem.at[g, j],
            )
            for j in range(2)
        ]
        for g in range(GROUPS)
    ]
    for pair in rows_in:
        for copy in pair:
            copy.start()

    def lead_copy(d, j):
        return pltpu.make_async_remote_copy(
            src_ref=lead.at[j], dst_ref=lead.at[j],
            send_sem=lead_send.at[d - 1, j], recv_sem=lead_recv.at[j],
            device_id={"aux": d}, device_id_type=pl.DeviceIdType.MESH,
        )

    @pl.when(aux == 0)
    def _():
        pl.semaphore_wait(barrier, 1 + NX - 1 + NAUX - 1 + z)
        for j in range(2):
            lead_in[j].wait()
        for j in range(2):
            for d in (1, 2, 3):
                lead_copy(d, j).start()

    @pl.when(aux != 0)
    def _():
        pl.semaphore_wait(barrier, 1 + NX - 1 + 1 + z)

    for of in range(NZ - 1):
        @pl.when(z > of)
        def _():
            pl.semaphore_signal(z_ready.at[z], inc=1, device_id=z_peer[of], device_id_type=pl.DeviceIdType.MESH)

    for copy in small_in:
        copy.wait()
    dens_in.wait()
    locals_ = []

    def picks(k, shape, axis):
        column = lax.broadcasted_iota(jnp.int32, shape, axis)
        slot = column // BLK
        target = jnp.zeros(shape, jnp.int32)
        for s in range(SLOTS):
            target = jnp.where(slot == s, jnp.full(shape, block_ids[k, 0, s] * BLK), target)
        target = jnp.where(slot < jnp.full(shape, counts[0, k]), target + lax.rem(column, BLK), -1)
        window = lax.broadcasted_iota(jnp.int32, (WINDOW, WIDTH) if axis else (WIDTH, WINDOW), 1 - axis)
        return jnp.where(window == target, 1.0, 0.0).astype(BF16)

    for k in range(SLABS):
        some_rows = jnp.dot(picks(k, (WIDTH, 1), 0), dens[...], preferred_element_type=F32).astype(BF16)
        block = jnp.dot(some_rows, picks(k, (1, WIDTH), 1), preferred_element_type=F32)
        locals_.append(block.astype(BF16))

    @pl.when(aux != 0)
    def _():
        for j in range(2):
            lead_copy(1, j).wait_recv()

    leading = jnp.concatenate([lead[j].reshape(SLABS * PANEL, 128) for j in range(2)], axis=1)
    a = lax.broadcasted_iota(jnp.int32, (SLABS * PANEL, SLABS * PANEL), 0)
    b = lax.broadcasted_iota(jnp.int32, (SLABS * PANEL, SLABS * PANEL), 1)
    weight = None
    for k in range(SLABS):
        sort = jnp.where((b == SLABS * (a - k * PANEL) + k) & (a // PANEL == k), 1.0, 0.0).astype(BF16)
        chosen = jnp.dot(sort, leading, preferred_element_type=F32).astype(BF16)
        term = lax.dot_general(locals_[k], chosen, NT, preferred_element_type=F32)
        weight = term if weight is None else weight + term
    high = weight.astype(BF16)
    weights[:, : SLABS * PANEL] = high
    weights[:, SLABS * PANEL :] = (weight - high.astype(F32)).astype(BF16)

    left = lax.broadcasted_iota(jnp.int32, (TILE, 128), 1) < PANEL

    def multiply(g):
        for d in range(NX):
            x_of = lax.rem(x + d, NX)
            slot_of = (g * NX + d) % 4
            strip = jnp.concatenate(
                [rows[g, j, x_of].reshape(SLABS * PAIR, 128) for j in range(2)], axis=1
            )
            y = jnp.dot(strip, weights[...], preferred_element_type=F32)
            product[slot_of] = y[:, :128] + y[:, 128:]
            for core_of, dest in ((1 - core, sibling_out), (core, own)):
                start = core_of * (SLABS * ROWS)

                def every_second(offset):
                    return product[slot_of, pl.ds(start + offset, TILE, SLABS), :]

                low = [every_second(k) for k in range(SLABS)]
                top = [every_second(SLABS * SHIFT + k) for k in range(SLABS)]
                dest[g, d] = jnp.where(left, low[0], top[1]) + pltpu.roll(
                    jnp.where(left, top[0], low[1]), PANEL, 1
                )

    def core_copy(g):
        return pltpu.make_async_remote_copy(
            src_ref=sibling_out.at[g], dst_ref=sibling_in.at[g],
            send_sem=c_send.at[g], recv_sem=c_recv.at[g],
            device_id=sibling, device_id_type=pl.DeviceIdType.MESH,
        )

    def x_copy(g, d):
        return pltpu.make_async_remote_copy(
            src_ref=x_out.at[g, d - 1], dst_ref=x_in.at[g, d - 1],
            send_sem=x_send.at[g, d - 1], recv_sem=x_recv.at[g, d - 1],
            device_id=x_peer[d], device_id_type=pl.DeviceIdType.MESH,
        )

    def z_copy(g, slot):
        return pltpu.make_async_remote_copy(
            src_ref=z_out.at[g], dst_ref=z_in.at[slot],
            send_sem=z_send.at[g], recv_sem=z_recv.at[slot],
            device_id={"orb": at(x, g, core)}, device_id_type=pl.DeviceIdType.MESH,
        )

    def z_slot(g):
        return lax.rem(z - g + 2 * NZ - 1, NZ)

    def add_sibling(g):
        for d in range(1, NX):
            x_out[g, d - 1] = (own[g, d] + sibling_in[g, d]).astype(BF16)

    def add_x(g):
        total = own[g, 0] + sibling_in[g, 0]
        for d in (1, 3, 2):
            x_copy(g, d).wait_recv()
            total = total + x_in[g, d - 1].astype(F32)
        totals[g] = total
        z_out[g] = total.astype(BF16)

        @pl.when(z < g)
        def _():
            pl.semaphore_wait(z_ready.at[g], 1)

        @pl.when(z != g)
        def _():
            z_copy(g, z_slot(g)).start()

    for pair in rows_in:
        for copy in pair:
            copy.wait()
    for step in range(len(BLOCKS) + C_LAG):
        fresh = BLOCKS[step] if step < len(BLOCKS) else ()
        ripe = BLOCKS[step - C_LAG] if 0 <= step - C_LAG < len(BLOCKS) else ()
        done = BLOCKS[step - C_LAG - X_LAG] if step >= C_LAG + X_LAG else ()
        for g in fresh:
            multiply(g)
            core_copy(g).start()
        for g in ripe:
            core_copy(g).wait_recv()
            add_sibling(g)
            for d in (2, 1, 3):
                x_copy(g, d).start()
        for g in done if fresh else ():
            add_x(g)
    for g in range(GROUPS - C_LAG - X_LAG, GROUPS):
        add_x(g)
    total = totals[z]
    for slot in range(NZ - 1):
        z_copy(0, slot).wait_recv()
        total = total + z_in[slot].astype(F32)
    total = total * (1.0 / math.sqrt(SLABS * NX * NZ * NC * WIDTH))
    turned = total.T
    out[:, :TILE] = turned[:PANEL]
    out[:, TILE:] = turned[PANEL:, TILE - SHIFT :]

    for g in range(GROUPS):
        core_copy(g).wait_send()
        for d in range(1, NX):
            x_copy(g, d).wait_send()

        @pl.when(z != g)
        def _():
            z_copy(g, z_slot(g)).wait_send()

    @pl.when(aux == 0)
    def _():
        for j in range(2):
            for d in range(1, NAUX):
                lead_copy(d, j).wait_send()


def on_device(tensor, density, block_ids, counts):
    tensor = tensor.reshape(NX, NZ, PAIR, SLABS, WIDTH)
    piece = (TILE, 128)
    return pl.pallas_call(
        kernel,
        out_shape=jax.ShapeDtypeStruct((PANEL, ROWS), F32),
        in_specs=[
            pl.BlockSpec(memory_space=pltpu.HBM),
            pl.BlockSpec(memory_space=pltpu.HBM),
            pl.BlockSpec(memory_space=pltpu.HBM),
            pl.BlockSpec(memory_space=pltpu.HBM),
        ],
        out_specs=pl.BlockSpec(memory_space=pltpu.VMEM),
        scratch_shapes=[
            pltpu.SMEM((SLABS, 1, SLOTS), jnp.int32),
            pltpu.SMEM((1, SLABS), jnp.int32),
            pltpu.SemaphoreType.DMA((2,)),
            pltpu.VMEM((GROUPS, 2, NX, PAIR, SLABS, 128), BF16),
            pltpu.VMEM((WINDOW, WINDOW), BF16),
            pltpu.VMEM((2, PANEL, SLABS, 128), BF16),
            pltpu.VMEM((WIDTH, 2 * SLABS * PANEL), BF16),
            pltpu.VMEM((4, SLABS * PAIR, 128), F32),
            pltpu.VMEM((GROUPS, NX) + piece, F32),
            pltpu.VMEM((GROUPS, NX) + piece, F32),
            pltpu.VMEM((GROUPS, NX) + piece, F32),
            pltpu.VMEM((GROUPS, NX - 1) + piece, BF16),
            pltpu.VMEM((GROUPS, NX - 1) + piece, BF16),
            pltpu.VMEM((GROUPS,) + piece, F32),
            pltpu.VMEM((GROUPS,) + piece, BF16),
            pltpu.VMEM((NZ,) + piece, BF16),
            pltpu.SemaphoreType.DMA((GROUPS, 2)),
            pltpu.SemaphoreType.DMA,
            pltpu.SemaphoreType.DMA((2,)),
            pltpu.SemaphoreType.DMA((NAUX - 1, 2)),
            pltpu.SemaphoreType.DMA((2,)),
            pltpu.SemaphoreType.REGULAR((NZ,)),
            pltpu.SemaphoreType.DMA((GROUPS,)),
            pltpu.SemaphoreType.DMA((GROUPS,)),
            pltpu.SemaphoreType.DMA((GROUPS, NX - 1)),
            pltpu.SemaphoreType.DMA((GROUPS, NX - 1)),
            pltpu.SemaphoreType.DMA((GROUPS,)),
            pltpu.SemaphoreType.DMA((NZ,)),
        ],
        compiler_params=pltpu.CompilerParams(
            collective_id=0, has_side_effects=True, vmem_limit_bytes=32 << 20
        ),
    )(*[pltpu.with_memory_space_constraint(a, pltpu.HBM) for a in (tensor, density, block_ids, counts.T)])


def solution(mesh):
    return jax.shard_map(
        on_device,
        mesh=mesh,
        in_specs=(
            P("aux", None, "orb", None),
            P("orb", None, None),
            P(None, "orb", None),
            P(None, "orb"),
        ),
        out_specs=P(None, ("aux", "orb")),
        check_vma=False,
    )
```

```python
import functools
import math

import jax
import jax.numpy as jnp
from jax import lax
from jax.experimental import pallas as pl
from jax.experimental.pallas import tpu as pltpu
from jax.sharding import PartitionSpec as P

PANEL = 64
NX, NZ, NC, NAUX = 4, 8, 2, 4
SLABS = 2
SLOTS = 4
BLK = 64
WIDTH = SLOTS * BLK
WINDOW = 512
ROWS = 120
PAIR = NC * ROWS
TILE = 64
SHIFT = ROWS - TILE
GROUPS = NZ
BLOCKS = ((0,), (1,), (2,), (3,), (4,), (5,), (6,), (7,))
C_LAG, X_LAG = 2, 4
F32, BF16 = jnp.float32, jnp.bfloat16
NT = (((1,), (1,)), ((), ()))


def kernel(
    tensor, density, block_ids_in, counts_in, out, block_ids, counts, small_sem,
    rows, dens, lead, weights, folded, own, sibling_out, sibling_in, x_out, x_in, totals, z_out, z_in,
    rows_sem, dens_sem, lead_sem, lead_send, lead_recv,
    z_ready, c_send, c_recv, x_send, x_recv, z_send, z_recv,
):
    orb, aux = lax.axis_index("orb"), lax.axis_index("aux")
    core = lax.rem(orb, NC)
    z = lax.rem(orb // NC, NZ)
    x = orb // (NC * NZ)

    def at(x_of, z_of, core_of):
        return (x_of * NZ + z_of) * NC + core_of

    sibling = {"orb": at(x, z, 1 - core)}
    x_peer = [{"orb": at(lax.rem(x + d, NX), z, core)} for d in range(NX)]
    z_peer = [{"orb": at(x, of, core)} for of in range(NZ)]

    barrier = pltpu.get_barrier_semaphore()

    @pl.when(aux == 0)
    def _():
        for d in range(1, NAUX):
            pl.semaphore_signal(barrier, inc=1, device_id={"aux": d}, device_id_type=pl.DeviceIdType.MESH)

    @pl.when(aux != 0)
    def _():
        pl.semaphore_signal(barrier, inc=1, device_id={"aux": 0}, device_id_type=pl.DeviceIdType.MESH)

    for peer in [sibling] + x_peer[1:]:
        pl.semaphore_signal(barrier, inc=1, device_id=peer, device_id_type=pl.DeviceIdType.MESH)
    for of in range(1, NZ):
        @pl.when(z < of)
        def _():
            pl.semaphore_signal(barrier, inc=1, device_id=z_peer[of], device_id_type=pl.DeviceIdType.MESH)

    lead_in = [
        pltpu.make_async_copy(
            tensor.at[0, 0, pl.ds(0, PANEL), :, pl.ds(128 * j, 128)], lead.at[j], lead_sem.at[j]
        )
        for j in range(2)
    ]

    @pl.when(aux == 0)
    def _():
        for copy in lead_in:
            copy.start()

    small_in = [
        pltpu.make_async_copy(block_ids_in, block_ids, small_sem.at[0]),
        pltpu.make_async_copy(counts_in, counts, small_sem.at[1]),
    ]
    for copy in small_in:
        copy.start()
    dens_in = pltpu.make_async_copy(density.at[0], dens, dens_sem)
    dens_in.start()
    rows_in = [
        [
            pltpu.make_async_copy(
                tensor.at[:, g, :, :, pl.ds(128 * j, 128)],
                rows.at[g, j],
                rows_sem.at[g, j],
            )
            for j in range(2)
        ]
        for g in range(GROUPS)
    ]
    for pair in rows_in:
        for copy in pair:
            copy.start()

    def lead_copy(d, j):
        return pltpu.make_async_remote_copy(
            src_ref=lead.at[j], dst_ref=lead.at[j],
            send_sem=lead_send.at[d - 1, j], recv_sem=lead_recv.at[j],
            device_id={"aux": d}, device_id_type=pl.DeviceIdType.MESH,
        )

    @pl.when(aux == 0)
    def _():
        pl.semaphore_wait(barrier, 1 + NX - 1 + NAUX - 1 + z)
        for j in range(2):
            lead_in[j].wait()
        for j in range(2):
            for d in (1, 2, 3):
                lead_copy(d, j).start()

    @pl.when(aux != 0)
    def _():
        pl.semaphore_wait(barrier, 1 + NX - 1 + 1 + z)

    for of in range(NZ - 1):
        @pl.when(z > of)
        def _():
            pl.semaphore_signal(z_ready.at[z], inc=1, device_id=z_peer[of], device_id_type=pl.DeviceIdType.MESH)

    for copy in small_in:
        copy.wait()
    dens_in.wait()
    locals_ = []

    def picks(k, shape, axis):
        column = lax.broadcasted_iota(jnp.int32, shape, axis)
        slot = column // BLK
        target = jnp.zeros(shape, jnp.int32)
        for s in range(SLOTS):
            target = jnp.where(slot == s, jnp.full(shape, block_ids[k, 0, s] * BLK), target)
        target = jnp.where(slot < jnp.full(shape, counts[0, k]), target + lax.rem(column, BLK), -1)
        window = lax.broadcasted_iota(jnp.int32, (WINDOW, WIDTH) if axis else (WIDTH, WINDOW), 1 - axis)
        return jnp.where(window == target, 1.0, 0.0).astype(BF16)

    for k in range(SLABS):
        some_rows = jnp.dot(picks(k, (WIDTH, 1), 0), dens[...], preferred_element_type=F32).astype(BF16)
        block = jnp.dot(some_rows, picks(k, (1, WIDTH), 1), preferred_element_type=F32)
        locals_.append(block.astype(BF16))

    @pl.when(aux != 0)
    def _():
        for j in range(2):
            lead_copy(1, j).wait_recv()

    leading = jnp.concatenate([lead[j].reshape(SLABS * PANEL, 128) for j in range(2)], axis=1)
    a = lax.broadcasted_iota(jnp.int32, (SLABS * PANEL, SLABS * PANEL), 0)
    b = lax.broadcasted_iota(jnp.int32, (SLABS * PANEL, SLABS * PANEL), 1)
    weight = None
    for k in range(SLABS):
        sort = jnp.where((b == SLABS * (a - k * PANEL) + k) & (a // PANEL == k), 1.0, 0.0).astype(BF16)
        chosen = jnp.dot(sort, leading, preferred_element_type=F32).astype(BF16)
        term = lax.dot_general(locals_[k], chosen, NT, preferred_element_type=F32)
        weight = term if weight is None else weight + term
    high = weight.astype(BF16)
    weights[:, : SLABS * PANEL] = high
    weights[:, SLABS * PANEL :] = (weight - high.astype(F32)).astype(BF16)

    left = lax.broadcasted_iota(jnp.int32, (TILE, 128), 1) < PANEL
    eights = (SLABS * PAIR // 16, 8, 128)
    half = lax.broadcasted_iota(jnp.int32, eights, 2) < PANEL
    even = lax.rem(lax.broadcasted_iota(jnp.int32, eights, 1), 2) == 0

    def multiply(g):
        for d in range(NX):
            x_of = lax.rem(x + d, NX)
            slot_of = (g * NX + d) % 4
            strip = jnp.concatenate(
                [rows[g, j, x_of].reshape(SLABS * PAIR, 128) for j in range(2)], axis=1
            )
            y = jnp.dot(strip, weights[...], preferred_element_type=F32)
            v = (y[:, :128] + y[:, 128:]).reshape(SLABS * PAIR // 16, 16, 128)
            v0, v1 = v[:, :8], v[:, 8:]
            up, down = pltpu.roll(v0, 7, 1), pltpu.roll(v1, 1, 1)
            fold = jnp.where(half, jnp.where(even, v0, down), jnp.where(even, up, v1)).reshape(PAIR, 128)
            folded[slot_of] = fold
            for core_of, dest in ((1 - core, sibling_out), (core, own)):
                base = core_of * ROWS
                low = folded[slot_of, pl.ds(base, TILE), :]
                top = folded[slot_of, pl.ds(base + SHIFT, TILE), :]
                dest[g, d] = jnp.where(left, low, top) + pltpu.roll(jnp.where(left, top, low), PANEL, 1)

    def core_copy(g):
        return pltpu.make_async_remote_copy(
            src_ref=sibling_out.at[g], dst_ref=sibling_in.at[g],
            send_sem=c_send.at[g], recv_sem=c_recv.at[g],
            device_id=sibling, device_id_type=pl.DeviceIdType.MESH,
        )

    def x_copy(g, d):
        return pltpu.make_async_remote_copy(
            src_ref=x_out.at[g, d - 1], dst_ref=x_in.at[g, d - 1],
            send_sem=x_send.at[g, d - 1], recv_sem=x_recv.at[g, d - 1],
            device_id=x_peer[d], device_id_type=pl.DeviceIdType.MESH,
        )

    def z_copy(g, slot):
        return pltpu.make_async_remote_copy(
            src_ref=z_out.at[g], dst_ref=z_in.at[slot],
            send_sem=z_send.at[g], recv_sem=z_recv.at[slot],
            device_id={"orb": at(x, g, core)}, device_id_type=pl.DeviceIdType.MESH,
        )

    def z_slot(g):
        return lax.rem(z - g + 2 * NZ - 1, NZ)

    def add_sibling(g):
        for d in range(1, NX):
            x_out[g, d - 1] = (own[g, d] + sibling_in[g, d]).astype(BF16)

    def add_x(g):
        total = own[g, 0] + sibling_in[g, 0]
        for d in (1, 3, 2):
            x_copy(g, d).wait_recv()
            total = total + x_in[g, d - 1].astype(F32)
        totals[g] = total
        z_out[g] = total.astype(BF16)

        @pl.when(z < g)
        def _():
            pl.semaphore_wait(z_ready.at[g], 1)

        @pl.when(z != g)
        def _():
            z_copy(g, z_slot(g)).start()

    for pair in rows_in:
        for copy in pair:
            copy.wait()
    for step in range(len(BLOCKS) + C_LAG):
        fresh = BLOCKS[step] if step < len(BLOCKS) else ()
        ripe = BLOCKS[step - C_LAG] if 0 <= step - C_LAG < len(BLOCKS) else ()
        done = BLOCKS[step - C_LAG - X_LAG] if step >= C_LAG + X_LAG else ()
        for g in fresh:
            multiply(g)
            core_copy(g).start()
        for g in ripe:
            core_copy(g).wait_recv()
            add_sibling(g)
            for d in (2, 1, 3):
                x_copy(g, d).start()
        for g in done if fresh else ():
            add_x(g)
    for g in range(GROUPS - C_LAG - X_LAG, GROUPS):
        add_x(g)
    total = totals[z]
    for slot in range(NZ - 1):
        z_copy(0, slot).wait_recv()
        total = total + z_in[slot].astype(F32)
    total = total * (1.0 / math.sqrt(SLABS * NX * NZ * NC * WIDTH))
    folded[0, :TILE] = total
    total = jnp.concatenate(
        [folded[0, pl.ds(k, TILE // 2, 2), :].reshape(TILE // 8, 4, 128) for k in range(2)], axis=1
    ).reshape(TILE, 128)
    turned = total.T
    out[:, :TILE] = turned[:PANEL]
    out[:, TILE:] = turned[PANEL:, TILE - SHIFT :]

    for g in range(GROUPS):
        core_copy(g).wait_send()
        for d in range(1, NX):
            x_copy(g, d).wait_send()

        @pl.when(z != g)
        def _():
            z_copy(g, z_slot(g)).wait_send()

    @pl.when(aux == 0)
    def _():
        for j in range(2):
            for d in range(1, NAUX):
                lead_copy(d, j).wait_send()


def on_device(tensor, density, block_ids, counts):
    tensor = tensor.reshape(NX, NZ, PAIR, SLABS, WIDTH)
    piece = (TILE, 128)
    return pl.pallas_call(
        kernel,
        out_shape=jax.ShapeDtypeStruct((PANEL, ROWS), F32),
        in_specs=[
            pl.BlockSpec(memory_space=pltpu.HBM),
            pl.BlockSpec(memory_space=pltpu.HBM),
            pl.BlockSpec(memory_space=pltpu.HBM),
            pl.BlockSpec(memory_space=pltpu.HBM),
        ],
        out_specs=pl.BlockSpec(memory_space=pltpu.VMEM),
        scratch_shapes=[
            pltpu.SMEM((SLABS, 1, SLOTS), jnp.int32),
            pltpu.SMEM((1, SLABS), jnp.int32),
            pltpu.SemaphoreType.DMA((2,)),
            pltpu.VMEM((GROUPS, 2, NX, PAIR, SLABS, 128), BF16),
            pltpu.VMEM((WINDOW, WINDOW), BF16),
            pltpu.VMEM((2, PANEL, SLABS, 128), BF16),
            pltpu.VMEM((WIDTH, 2 * SLABS * PANEL), BF16),
            pltpu.VMEM((4, PAIR, 128), F32),
            pltpu.VMEM((GROUPS, NX) + piece, F32),
            pltpu.VMEM((GROUPS, NX) + piece, F32),
            pltpu.VMEM((GROUPS, NX) + piece, F32),
            pltpu.VMEM((GROUPS, NX - 1) + piece, BF16),
            pltpu.VMEM((GROUPS, NX - 1) + piece, BF16),
            pltpu.VMEM((GROUPS,) + piece, F32),
            pltpu.VMEM((GROUPS,) + piece, BF16),
            pltpu.VMEM((NZ,) + piece, BF16),
            pltpu.SemaphoreType.DMA((GROUPS, 2)),
            pltpu.SemaphoreType.DMA,
            pltpu.SemaphoreType.DMA((2,)),
            pltpu.SemaphoreType.DMA((NAUX - 1, 2)),
            pltpu.SemaphoreType.DMA((2,)),
            pltpu.SemaphoreType.REGULAR((NZ,)),
            pltpu.SemaphoreType.DMA((GROUPS,)),
            pltpu.SemaphoreType.DMA((GROUPS,)),
            pltpu.SemaphoreType.DMA((GROUPS, NX - 1)),
            pltpu.SemaphoreType.DMA((GROUPS, NX - 1)),
            pltpu.SemaphoreType.DMA((GROUPS,)),
            pltpu.SemaphoreType.DMA((NZ,)),
        ],
        compiler_params=pltpu.CompilerParams(
            collective_id=0, has_side_effects=True, vmem_limit_bytes=32 << 20
        ),
    )(*[pltpu.with_memory_space_constraint(a, pltpu.HBM) for a in (tensor, density, block_ids, counts.T)])


def solution(mesh):
    return jax.shard_map(
        on_device,
        mesh=mesh,
        in_specs=(
            P("aux", None, "orb", None),
            P("orb", None, None),
            P(None, "orb", None),
            P(None, "orb"),
        ),
        out_specs=P(None, ("aux", "orb")),
        check_vma=False,
    )
```
